32 devices in a mesh: fsdp: 4 (over z), tensor: 8 (over y, x, core).
Axes of the slice: x: 2, y: 2, z: 4, core: 2. Of those that a mesh axis runs over, the one named last changes fastest.
Arguments:
- val_x: bfloat16 [2048, 8192], P('fsdp', 'tensor'), may hold values from -6 to 6
- val_cot: bfloat16 [2048, 16384], P('fsdp', 'tensor'), may hold values from -0.0014648438 to 0.0014648438
- second_moment: float32 [8192, 16384], P('fsdp', 'tensor'), may hold values from 0.01 to 1
- train_x: bfloat16 [1024, 8192], P('fsdp', 'tensor'), may hold values from -6 to 6
- train_cot: bfloat16 [1024, 16384], P('fsdp', 'tensor'), may hold values from -0.046875 to 0.046875
Outputs:
- scores: float32 [1024], P('fsdp')
The draws below stay inside these ranges and needn't reach their ends.
All inputs are finite; a program needn't handle non-finite values.
Results may differ from the reference program's by a relative error of at most 0.019.
Values may be sent and summed in bfloat16 or wider, within the bound.
A program may use at most 128 MiB of HBM per device.

```python
import math
import jax
import jax.numpy as jnp
from jax import lax

D = 8192
FF = 16384
VT_DEV = 512
VTOKENS = 2048
TTOKENS = 1024
N_FSDP = 4


def spiked(entries, own_key, source, target, blocks, factor):
    def block_of(position):
        return (jnp.arange(entries.shape[position]) // (entries.shape[position] // blocks)).reshape((-1,) + (1,) * (entries.ndim - 1 - position))

    one_side = jax.random.permutation(own_key, blocks)[block_of(target)]
    far = (block_of(target) + blocks // 2) % blocks
    return jnp.where((block_of(source) == one_side) | (block_of(source) == far), factor * entries, entries)


def steps_of(rng, shape, cuts, least, largest):
    level = 1.0
    for position, parts in cuts:
        heights = jax.random.uniform(jax.random.fold_in(jax.random.fold_in(rng, 6), position), (parts,), jnp.float32, least / len(cuts), largest / len(cuts))
        level = level * jnp.repeat(jnp.exp(heights), shape[position] // parts).reshape((-1,) + (1,) * (len(shape) - 1 - position))
    return level


def scatter_about(rng, extent, width, bound, cuts=(), kind=jnp.bfloat16):
    drawn = width * jax.random.normal(rng, extent, jnp.float32)
    if cuts:
        drawn = drawn * steps_of(rng, extent, cuts, -0.22, 0.18)
    return jnp.clip(drawn, -bound, bound).astype(kind)


def noise_with(rng, dims, width, bound, pieces, heavy, held_as=jnp.bfloat16):
    result = width * jax.random.normal(rng, dims, jnp.float32)
    if pieces:
        result = result * steps_of(rng, dims, pieces, -0.22, 0.18)
    return jnp.clip(spiked(result, jax.random.fold_in(rng, 3), *heavy), -bound, bound).astype(held_as)


def setup_inputs(seed: int = 0) -> dict:
    seeds = jax.random.split(jax.random.key(seed), 6)
    val_x = noise_with(seeds[0], (VTOKENS, D), 1.0, 6.0, ((0, 4), (1, 8)), (0, 1, 8, 2.0))
    val_cot = scatter_about(seeds[1], (VTOKENS, FF), (1.0 / (VTOKENS * D) ** 0.5), 0.0014648438, ((0, 4), (1, 8)))
    second_moment = jnp.clip(jnp.exp(math.log(1.0) - 4.6051702 * jax.random.uniform(seeds[2], (D, FF), jnp.float32) ** steps_of(seeds[2], (D, FF), ((0, 4), (1, 8)), -0.2, 0.2)), 0.01, 1.0)
    train_x = scatter_about(seeds[3], (TTOKENS, D), 1.0, 6.0, ((0, 4), (1, 8)))
    train_cot = scatter_about(seeds[4], (TTOKENS, FF), FF ** -0.5, 0.046875, ((0, 4), (1, 8)))
    return dict(val_x=val_x, val_cot=val_cot, second_moment=second_moment, train_x=train_x, train_cot=train_cot)


EPSILON = 1e-08

def reference(val_x, val_cot, second_moment, train_x, train_cot):
    groups_x = val_x.reshape(N_FSDP, VT_DEV, D)
    groups_c = val_cot.reshape(N_FSDP, VT_DEV, FF)

    def add_group(total, pair):
        part = lax.dot_general(pair[0], pair[1], (((0,), (0,)), ((), ())), preferred_element_type=jnp.float32)
        part = lax.optimization_barrier(part.astype(jnp.bfloat16))
        return (total + part.astype(jnp.float32), None)
    grad, _ = lax.scan(add_group, jnp.zeros((D, FF), jnp.float32), (groups_x, groups_c))
    delta = (grad / (jnp.sqrt(second_moment) + EPSILON)).astype(jnp.bfloat16)
    shifted = jnp.dot(train_x, delta, preferred_element_type=jnp.float32)
    return lax.optimization_barrier(jnp.sum(shifted * train_cot.astype(jnp.float32), axis=1))
```

```python
import jax
import jax.numpy as jnp
from jax import lax
from jax.sharding import PartitionSpec as P

EPSILON = 1e-08


def rows_of_block(x):
    n_tensor, n_fsdp = lax.axis_size("tensor"), lax.axis_size("fsdp")
    share = x.shape[0] // n_tensor
    spread = lax.all_to_all(x, "tensor", split_axis=0, concat_axis=1, tiled=True)
    moved = lax.all_to_all(spread, "fsdp", split_axis=1, concat_axis=0, tiled=True)
    whole = lax.all_gather(moved, "tensor", axis=0, tiled=True)
    rows = whole.shape[1]
    whole = whole.reshape(n_tensor, n_fsdp, share, rows)
    return whole.transpose(1, 0, 2, 3).reshape(n_fsdp * n_tensor * share, rows)


def per_device(val_x, val_cot, second_moment, train_x, train_cot):
    all_cot = lax.all_gather(val_cot, "fsdp", axis=0, tiled=True)
    all_train_cot = lax.all_gather(train_cot, "fsdp", axis=0, tiled=True)
    x_rows = rows_of_block(val_x)
    train_rows = rows_of_block(train_x)
    grad = lax.dot_general(
        x_rows, all_cot, (((0,), (0,)), ((), ())), preferred_element_type=jnp.float32
    )
    delta = (grad / (jnp.sqrt(second_moment) + EPSILON)).astype(jnp.bfloat16)
    shifted = jnp.dot(train_rows, delta, preferred_element_type=jnp.float32)
    block_scores = jnp.sum(shifted * all_train_cot.astype(jnp.float32), axis=1)
    partial_scores = lax.psum_scatter(block_scores, "fsdp", scatter_dimension=0, tiled=True)
    return lax.psum(partial_scores, "tensor")


def solution(mesh):
    return jax.shard_map(
        per_device,
        mesh=mesh,
        in_specs=(P("fsdp", "tensor"),) * 5,
        out_specs=P("fsdp"),
        check_vma=False,
    )
```

```python
import functools

import jax
import jax.numpy as jnp
from jax import lax
from jax.experimental import pallas as pl
from jax.experimental.pallas import tpu as pltpu
from jax.sharding import PartitionSpec as P

EPSILON = 1e-08
CHUNK = 256
MESH = pl.DeviceIdType.MESH


def kernel(
    n_fsdp, n_tensor,
    val_x, val_cot, moment, train_x, train_cot, out,
    spread, spread_t, x_all, t_all, x_turned, cot, cot_t, moment_v, shifted, total,
    part, first, second,
    a_send, a_recv, b_send, b_recv, c_send, c_recv, up_send, down_send, cot_recv,
    moment_sem, own_sem, local_sem, r1_send, r1_recv, r2_send, r2_recv,
):
    z, t = lax.axis_index("fsdp"), lax.axis_index("tensor")
    chunks = cot.shape[0]
    depth, depth_t = val_cot.shape[0], train_cot.shape[0]
    rows, features = moment.shape[0], val_x.shape[1]
    share, share_t = spread.shape[0], spread_t.shape[0]

    def on_tensor(d):
        return lax.rem(t + d, n_tensor)

    def on_fsdp(d):
        return lax.rem(z + d, n_fsdp)

    def remote(src, dst, send, recv, device):
        return pltpu.make_async_remote_copy(
            src_ref=src, dst_ref=dst, send_sem=send, recv_sem=recv,
            device_id=device, device_id_type=MESH,
        )

    def loop(low, high, body):
        def step(i, carry):
            body(i)
            return carry
        lax.fori_loop(low, high, step, 0)

    barrier = pltpu.get_barrier_semaphore()

    @functools.partial(loop, 1, n_tensor)
    def _(d):
        pl.semaphore_signal(barrier, 1, device_id={"tensor": on_tensor(d)}, device_id_type=MESH)

    @functools.partial(loop, 1, n_fsdp)
    def _(d):
        pl.semaphore_signal(barrier, 1, device_id={"fsdp": on_fsdp(d)}, device_id_type=MESH)

    pl.semaphore_wait(barrier, n_tensor + n_fsdp - 2)

    def a_copies(peer, owner, d):
        columns = pl.ds(pl.multiple_of(owner * features, features), features)
        return (
            remote(val_x.at[pl.ds(pl.multiple_of(peer * share, share), share)],
                   spread.at[:, columns], a_send.at[0, d], a_recv.at[0, owner], {"tensor": peer}),
            remote(train_x.at[pl.ds(pl.multiple_of(peer * share_t, share_t), share_t)],
                   spread_t.at[:, columns], a_send.at[1, d], a_recv.at[1, owner], {"tensor": peer}),
        )

    def a_own():
        columns = pl.ds(pl.multiple_of(t * features, features), features)
        return (
            pltpu.make_async_copy(val_x.at[pl.ds(pl.multiple_of(t * share, share), share)],
                                  spread.at[:, columns], local_sem.at[0]),
            pltpu.make_async_copy(train_x.at[pl.ds(pl.multiple_of(t * share_t, share_t), share_t)],
                                  spread_t.at[:, columns], local_sem.at[1]),
        )

    def b_copies(peer, owner, d):
        columns = pl.ds(pl.multiple_of(peer * rows, rows), rows)
        return (
            remote(spread.at[:, columns],
                   x_all.at[owner, pl.ds(pl.multiple_of(t * share, share), share)],
                   b_send.at[0, d], b_recv.at[0, owner], {"fsdp": peer}),
            remote(spread_t.at[:, columns],
                   t_all.at[owner, pl.ds(pl.multiple_of(t * share_t, share_t), share_t)],
                   b_send.at[1, d], b_recv.at[1, owner], {"fsdp": peer}),
        )

    def b_own():
        columns = pl.ds(pl.multiple_of(z * rows, rows), rows)
        return (
            pltpu.make_async_copy(
                spread.at[:, columns],
                x_all.at[z, pl.ds(pl.multiple_of(t * share, share), share)], local_sem.at[0]),
            pltpu.make_async_copy(
                spread_t.at[:, columns],
                t_all.at[z, pl.ds(pl.multiple_of(t * share_t, share_t), share_t)],
                local_sem.at[1]),
        )

    def c_copies(peer, owner, d):
        piece = pl.ds(pl.multiple_of(owner * share, share), share)
        piece_t = pl.ds(pl.multiple_of(owner * share_t, share_t), share_t)
        return (
            remote(x_all.at[:, piece], x_all.at[:, piece],
                   c_send.at[0, d], c_recv.at[0, owner], {"tensor": peer}),
            remote(t_all.at[:, piece_t], t_all.at[:, piece_t],
                   c_send.at[1, d], c_recv.at[1, owner], {"tensor": peer}),
        )

    def cot_places(shard, c):
        return (cot.at[c, pl.ds(pl.multiple_of(shard * depth, depth), depth)],
                cot_t.at[c, pl.ds(pl.multiple_of(shard * depth_t, depth_t), depth_t)])

    def cot_copies(shard, c, sems, peer, own):
        places = cot_places(shard, c)
        columns = pl.ds(pl.multiple_of(c * CHUNK, CHUNK), CHUNK)
        sources = (val_cot.at[:, columns], train_cot.at[:, columns]) if own else places
        return tuple(
            remote(sources[i], places[i], sems.at[i, shard, c], cot_recv.at[i, shard, c],
                   {"fsdp": peer})
            for i in range(2)
        )

    below, above = lax.max(z - 1, 0), lax.min(z + 1, n_fsdp - 1)

    def start_cot(shard, c, own):
        @pl.when(z < n_fsdp - 1)
        def _():
            if own:
                for copy in cot_copies(shard, c, up_send, above, own):
                    copy.start()
        @pl.when(z > 0)
        def _():
            if own:
                for copy in cot_copies(shard, c, down_send, below, own):
                    copy.start()

    def cot_own(c):
        columns = pl.ds(pl.multiple_of(c * CHUNK, CHUNK), CHUNK)
        places = cot_places(z, c)
        return (
            pltpu.make_async_copy(val_cot.at[:, columns], places[0], own_sem.at[0, c]),
            pltpu.make_async_copy(train_cot.at[:, columns], places[1], own_sem.at[1, c]),
        )

    def moment_copy(c):
        columns = pl.ds(pl.multiple_of(c * CHUNK, CHUNK), CHUNK)
        return pltpu.make_async_copy(moment.at[:, columns], moment_v.at[c], moment_sem.at[c])

    @functools.partial(loop, 1, n_tensor)
    def _(d):
        for copy in a_copies(on_tensor(d), t, d):
            copy.start()

    for copy in a_own():
        copy.start()
    early = 1
    loop(0, early, lambda c: start_cot(z, c, True))

    @functools.partial(loop, 1, n_tensor)
    def _(d):
        owner = on_tensor(d)
        for copy in a_copies(owner, owner, d):
            copy.wait_recv()

    for copy in a_own():
        copy.wait()

    @functools.partial(loop, 1, n_fsdp)
    def _(d):
        for copy in b_copies(on_fsdp(d), z, d):
            copy.start()

    for copy in b_own():
        copy.start()
    loop(early, chunks, lambda c: start_cot(z, c, True))

    @functools.partial(loop, 0, chunks)
    def _(c):
        for copy in cot_own(c):
            copy.start()
        moment_copy(c).start()

    @functools.partial(loop, 1, n_fsdp)
    def _(d):
        owner = on_fsdp(d)
        for copy in b_copies(owner, owner, d):
            copy.wait_recv()

    for copy in b_own():
        copy.wait()

    @functools.partial(loop, 1, n_tensor)
    def _(d):
        for copy in c_copies(on_tensor(d), t, d):
            copy.start()

    def pass_on(k, c):
        lower, upper = z - k, z + k

        @pl.when(lower >= 0)
        def _():
            copies = cot_copies(lower, c, up_send, above, False)
            for copy in copies:
                copy.wait_recv()

            @pl.when(z < n_fsdp - 1)
            def _():
                for copy in copies:
                    copy.start()

        @pl.when(upper < n_fsdp)
        def _():
            copies = cot_copies(upper, c, down_send, below, False)
            for copy in copies:
                copy.wait_recv()

            @pl.when(z > 0)
            def _():
                for copy in copies:
                    copy.start()

    @functools.partial(loop, 1, n_fsdp - 1)
    def _(k):
        loop(0, chunks, lambda c: pass_on(k, c))

    @functools.partial(loop, 1, n_tensor)
    def _(d):
        owner = on_tensor(d)
        for copy in c_copies(owner, owner, d):
            copy.wait_recv()

    tile = 256

    @functools.partial(loop, 0, rows // tile)
    def _(i):
        columns = pl.ds(pl.multiple_of(i * tile, tile), tile)
        for group in range(n_fsdp):
            x_turned[columns, group * depth:(group + 1) * depth] = x_all[group, :, columns].T

    total[...] = jnp.zeros_like(total)

    @functools.partial(loop, 0, chunks)
    def _(c):
        pass_on(n_fsdp - 1, c)
        for copy in cot_own(c):
            copy.wait()
        moment_copy(c).wait()
        shifted[...] = jnp.zeros_like(shifted)

        @functools.partial(loop, 0, rows // tile)
        def _(i):
            block = pl.ds(pl.multiple_of(i * tile, tile), tile)
            grad = jnp.dot(x_turned[block, :], cot[c], preferred_element_type=jnp.float32)
            delta = (grad / (jnp.sqrt(moment_v[c, block, :]) + EPSILON)).astype(jnp.bfloat16)
            lhs = t_all[:, :, block].reshape(n_fsdp * depth_t, tile)
            shifted[...] += jnp.dot(lhs, delta, preferred_element_type=jnp.float32)

        scored = shifted[...] * cot_t[c].astype(jnp.float32)
        folded = scored[:, :128]
        for low in range(128, CHUNK, 128):
            folded = folded + scored[:, low:low + 128]
        total[...] += folded

    for block in range(n_fsdp):
        turned = total[block * depth_t:(block + 1) * depth_t, :].T
        part[block] = jnp.sum(turned.reshape(16, 8, depth_t), axis=0)

    def r1_copy(peer, owner, d):
        return remote(part.at[peer], first.at[owner], r1_send.at[d], r1_recv.at[owner],
                      {"fsdp": peer})

    @functools.partial(loop, 1, n_fsdp)
    def _(d):
        r1_copy(on_fsdp(d), z, d).start()

    first[z] = part[z]

    @functools.partial(loop, 1, n_fsdp)
    def _(d):
        owner = on_fsdp(d)
        r1_copy(owner, owner, d).wait_recv()

    second[t] = jnp.sum(first[...], axis=0)

    def r2_copy(peer, owner, d):
        return remote(second.at[owner], second.at[owner], r2_send.at[d], r2_recv.at[owner],
                      {"tensor": peer})

    @functools.partial(loop, 1, n_tensor)
    def _(d):
        r2_copy(on_tensor(d), t, d).start()

    @functools.partial(loop, 1, n_tensor)
    def _(d):
        owner = on_tensor(d)
        r2_copy(owner, owner, d).wait_recv()

    out[...] = jnp.sum(jnp.sum(second[...], axis=0), axis=0, keepdims=True)

    @functools.partial(loop, 1, n_tensor)
    def _(d):
        peer = on_tensor(d)
        for copy in a_copies(peer, t, d) + c_copies(peer, t, d) + (r2_copy(peer, t, d),):
            copy.wait_send()

    @functools.partial(loop, 1, n_fsdp)
    def _(d):
        peer = on_fsdp(d)
        for copy in b_copies(peer, z, d) + (r1_copy(peer, z, d),):
            copy.wait_send()

    @functools.partial(loop, 0, n_fsdp)
    def _(shard):
        @pl.when((shard <= z) & (z < n_fsdp - 1))
        def _():
            @functools.partial(loop, 0, chunks)
            def _(c):
                for copy in cot_copies(shard, c, up_send, above, False):
                    copy.wait_send()

        @pl.when((shard >= z) & (z > 0))
        def _():
            @functools.partial(loop, 0, chunks)
            def _(c):
                for copy in cot_copies(shard, c, down_send, below, False):
                    copy.wait_send()


def per_device(n_fsdp, n_tensor, val_x, val_cot, second_moment, train_x, train_cot):
    depth, depth_t = val_x.shape[0], train_x.shape[0]
    rows, hidden = second_moment.shape
    chunks = hidden // CHUNK
    width = val_x.shape[1] * n_tensor
    bf16, f32 = jnp.bfloat16, jnp.float32
    dma = pltpu.SemaphoreType.DMA
    scores = pl.pallas_call(
        functools.partial(kernel, n_fsdp, n_tensor),
        out_shape=jax.ShapeDtypeStruct((1, depth_t), f32),
        in_specs=[pl.BlockSpec(memory_space=pl.ANY)] * 5,
        out_specs=pl.BlockSpec(memory_space=pltpu.VMEM),
        scratch_shapes=[
            pltpu.VMEM((depth // n_tensor, width), bf16),
            pltpu.VMEM((depth_t // n_tensor, width), bf16),
            pltpu.VMEM((n_fsdp, depth, rows), bf16),
            pltpu.VMEM((n_fsdp, depth_t, rows), bf16),
            pltpu.VMEM((rows, n_fsdp * depth), bf16),
            pltpu.VMEM((chunks, n_fsdp * depth, CHUNK), bf16),
            pltpu.VMEM((chunks, n_fsdp * depth_t, CHUNK), bf16),
            pltpu.VMEM((chunks, rows, CHUNK), f32),
            pltpu.VMEM((n_fsdp * depth_t, CHUNK), f32),
            pltpu.VMEM((n_fsdp * depth_t, 128), f32),
            pltpu.VMEM((n_fsdp, 8, depth_t), f32),
            pltpu.VMEM((n_fsdp, 8, depth_t), f32),
            pltpu.VMEM((n_tensor, 8, depth_t), f32),
            dma((2, n_tensor)), dma((2, n_tensor)),
            dma((2, n_fsdp)), dma((2, n_fsdp)),
            dma((2, n_tensor)), dma((2, n_tensor)),
            dma((2, n_fsdp, chunks)), dma((2, n_fsdp, chunks)), dma((2, n_fsdp, chunks)),
            dma((chunks,)), dma((2, chunks)), dma((2,)),
            dma((n_fsdp,)), dma((n_fsdp,)), dma((n_tensor,)), dma((n_tensor,)),
        ],
        compiler_params=pltpu.CompilerParams(
            collective_id=0, has_side_effects=True, vmem_limit_bytes=60 * 1024 * 1024
        ),
        name="scores",
    )(val_x, val_cot, second_moment, train_x, train_cot)
    return scores.reshape(depth_t)


def solution(mesh):
    return jax.shard_map(
        functools.partial(per_device, mesh.shape["fsdp"], mesh.shape["tensor"]),
        mesh=mesh,
        in_specs=(P("fsdp", "tensor"),) * 5,
        out_specs=P("fsdp"),
        check_vma=False,
    )
```

```python
import functools

import jax
import jax.numpy as jnp
from jax import lax
from jax.experimental import pallas as pl
from jax.experimental.pallas import tpu as pltpu
from jax.sharding import PartitionSpec as P

EPSILON = 1e-08
CHUNK = 256
AHEAD = 2
MESH = pl.DeviceIdType.MESH


def kernel(
    n_fsdp, n_tensor,
    val_x, val_cot, moment, train_x, train_cot, out,
    spread, spread_t, x_all, t_all, x_turned, cot, cot_t, moment_v, shifted, total,
    up_in, down_in, second,
    a_send, a_recv, b_send, b_recv, c_send, c_recv, twin_send, up_send, down_send, cot_recv,
    rise_send, rise_recv, fall_send, fall_recv,
    moment_sem, own_sem, local_sem, r2_send, r2_recv,
):
    z, t = lax.axis_index("fsdp"), lax.axis_index("tensor")
    chunks = cot.shape[0]
    depth, depth_t = val_cot.shape[0], train_cot.shape[0]
    rows, features = moment.shape[0], val_x.shape[1]
    share, share_t = spread.shape[0], spread_t.shape[0]

    def on_tensor(d):
        return lax.rem(t + d, n_tensor)

    def on_fsdp(d):
        return lax.rem(z + d, n_fsdp)

    def remote(src, dst, send, recv, device):
        return pltpu.make_async_remote_copy(
            src_ref=src, dst_ref=dst, send_sem=send, recv_sem=recv,
            device_id=device, device_id_type=MESH,
        )

    def loop(low, high, body):
        def step(i, carry):
            body(i)
            return carry
        lax.fori_loop(low, high, step, 0)

    barrier = pltpu.get_barrier_semaphore()

    @functools.partial(loop, 1, n_tensor)
    def _(d):
        pl.semaphore_signal(barrier, 1, device_id={"tensor": on_tensor(d)}, device_id_type=MESH)

    @functools.partial(loop, 1, n_fsdp)
    def _(d):
        pl.semaphore_signal(barrier, 1, device_id={"fsdp": on_fsdp(d)}, device_id_type=MESH)

    pl.semaphore_wait(barrier, n_tensor + n_fsdp - 2)

    def a_copies(peer, owner, d):
        columns = pl.ds(pl.multiple_of(owner * features, features), features)
        return (
            remote(val_x.at[pl.ds(pl.multiple_of(peer * share, share), share)],
                   spread.at[:, columns], a_send.at[0, d], a_recv.at[0, owner], {"tensor": peer}),
            remote(train_x.at[pl.ds(pl.multiple_of(peer * share_t, share_t), share_t)],
                   spread_t.at[:, columns], a_send.at[1, d], a_recv.at[1, owner], {"tensor": peer}),
        )

    def a_own():
        columns = pl.ds(pl.multiple_of(t * features, features), features)
        return (
            pltpu.make_async_copy(val_x.at[pl.ds(pl.multiple_of(t * share, share), share)],
                                  spread.at[:, columns], local_sem.at[0]),
            pltpu.make_async_copy(train_x.at[pl.ds(pl.multiple_of(t * share_t, share_t), share_t)],
                                  spread_t.at[:, columns], local_sem.at[1]),
        )

    def b_copies(peer, owner, d):
        columns = pl.ds(pl.multiple_of(peer * rows, rows), rows)
        return (
            remote(spread.at[:, columns],
                   x_all.at[owner, pl.ds(pl.multiple_of(t * share, share), share)],
                   b_send.at[0, d], b_recv.at[0, owner], {"fsdp": peer}),
            remote(spread_t.at[:, columns],
                   t_all.at[owner, pl.ds(pl.multiple_of(t * share_t, share_t), share_t)],
                   b_send.at[1, d], b_recv.at[1, owner], {"fsdp": peer}),
        )

    def b_own():
        columns = pl.ds(pl.multiple_of(z * rows, rows), rows)
        return (
            pltpu.make_async_copy(
                spread.at[:, columns],
                x_all.at[z, pl.ds(pl.multiple_of(t * share, share), share)], local_sem.at[0]),
            pltpu.make_async_copy(
                spread_t.at[:, columns],
                t_all.at[z, pl.ds(pl.multiple_of(t * share_t, share_t), share_t)],
                local_sem.at[1]),
        )

    core = lax.rem(t, 2)
    twin = t + 1 - 2 * core
    pairs = n_tensor // 2

    def same_core(d):
        return 2 * lax.rem(t // 2 + d, pairs) + core

    def c_copy(i, peer, owner, sem):
        held, size = ((x_all, share), (t_all, share_t))[i]
        piece = pl.ds(pl.multiple_of(owner * size, size), size)
        return remote(held.at[:, piece], held.at[:, piece], sem, c_recv.at[i, owner],
                      {"tensor": peer})

    def c_start(i):
        @functools.partial(loop, 1, pairs)
        def _(d):
            c_copy(i, same_core(d), t, c_send.at[i, d]).start()

        c_copy(i, twin, t, twin_send.at[i, t]).start()

    def c_pass(i):
        @functools.partial(loop, 1, pairs)
        def _(d):
            owner = same_core(d)
            c_copy(i, owner, owner, c_send.at[i, d]).wait_recv()
            c_copy(i, twin, owner, twin_send.at[i, owner]).start()

    def c_finish(i):
        @functools.partial(loop, 0, pairs)
        def _(d):
            owner = same_core(d) + 1 - 2 * core
            c_copy(i, twin, owner, twin_send.at[i, owner]).wait_recv()

    def cot_copy(shard, c, sems, peer, own):
        place = cot.at[c, pl.ds(pl.multiple_of(shard * depth, depth), depth)]
        columns = pl.ds(pl.multiple_of(c * CHUNK, CHUNK), CHUNK)
        return remote(val_cot.at[:, columns] if own else place, place,
                      sems.at[shard, c], cot_recv.at[shard, c], {"fsdp": peer})

    below, above = lax.max(z - 1, 0), lax.min(z + 1, n_fsdp - 1)

    def start_own(c):
        @pl.when(z < n_fsdp - 1)
        def _():
            cot_copy(z, c, up_send, above, True).start()

        @pl.when(z > 0)
        def _():
            cot_copy(z, c, down_send, below, True).start()

    def cot_own(c):
        columns = pl.ds(pl.multiple_of(c * CHUNK, CHUNK), CHUNK)
        place = cot.at[c, pl.ds(pl.multiple_of(z * depth, depth), depth)]
        return (
            pltpu.make_async_copy(val_cot.at[:, columns], place, own_sem.at[0, c]),
            pltpu.make_async_copy(train_cot.at[:, columns], cot_t.at[c], own_sem.at[1, c]),
        )

    def moment_copy(c):
        columns = pl.ds(pl.multiple_of(c * CHUNK, CHUNK), CHUNK)
        return pltpu.make_async_copy(moment.at[:, columns], moment_v.at[lax.rem(c, 2)],
                                     moment_sem.at[lax.rem(c, 2)])

    @functools.partial(loop, 1, n_tensor)
    def _(d):
        for copy in a_copies(on_tensor(d), t, d):
            copy.start()

    for copy in a_own():
        copy.start()
    start_own(0)

    @functools.partial(loop, 1, n_tensor)
    def _(d):
        owner = on_tensor(d)
        for copy in a_copies(owner, owner, d):
            copy.wait_recv()

    for copy in a_own():
        copy.wait()

    @functools.partial(loop, 1, n_fsdp)
    def _(d):
        for copy in b_copies(on_fsdp(d), z, d):
            copy.start()

    for copy in b_own():
        copy.start()
    loop(1, AHEAD, start_own)

    @functools.partial(loop, 0, chunks)
    def _(c):
        for copy in cot_own(c):
            copy.start()

    for c in range(2):
        moment_copy(c).start()

    @functools.partial(loop, 1, n_fsdp)
    def _(d):
        owner = on_fsdp(d)
        for copy in b_copies(owner, owner, d):
            copy.wait_recv()

    for copy in b_own():
        copy.wait()

    c_start(0)
    c_start(1)

    def pass_on(k, c):
        lower, upper = z - k, z + k

        @pl.when(lower >= 0)
        def _():
            copy = cot_copy(lower, c, up_send, above, False)
            copy.wait_recv()

            @pl.when(z < n_fsdp - 1)
            def _():
                copy.start()

        @pl.when(upper < n_fsdp)
        def _():
            copy = cot_copy(upper, c, down_send, below, False)
            copy.wait_recv()

            @pl.when(z > 0)
            def _():
                copy.start()

    tile = 256

    def turn():
        @functools.partial(loop, 0, rows // tile)
        def _(i):
            columns = pl.ds(pl.multiple_of(i * tile, tile), tile)
            for group in range(n_fsdp):
                x_turned[columns, group * depth:(group + 1) * depth] = x_all[group, :, columns].T

    def rise_copy(c, block):
        return remote(up_in.at[c, block], up_in.at[c, block],
                      rise_send.at[c, block], rise_recv.at[c, block], {"fsdp": above})

    def fall_copy(c, block):
        return remote(down_in.at[c, block], down_in.at[c, block],
                      fall_send.at[c, block], fall_recv.at[c, block], {"fsdp": below})

    def own_part(c, block):
        return shifted[c, pl.ds(pl.multiple_of(block * depth_t, depth_t), depth_t), :]

    def compute(c):
        for copy in cot_own(c):
            copy.wait()
        moment_copy(c).wait()
        shifted[c] = jnp.zeros(shifted.shape[1:], jnp.float32)

        @functools.partial(loop, 0, rows // tile)
        def _(i):
            block = pl.ds(pl.multiple_of(i * tile, tile), tile)
            grad = jnp.dot(x_turned[block, :], cot[c], preferred_element_type=jnp.float32)
            root = jnp.sqrt(moment_v[lax.rem(c, 2), block, :]) + EPSILON
            delta = (grad / root).astype(jnp.bfloat16)
            lhs = t_all[:, :, block].reshape(n_fsdp * depth_t, tile)
            shifted[c] += jnp.dot(lhs, delta, preferred_element_type=jnp.float32)

        @pl.when(c + 2 < chunks)
        def _():
            moment_copy(c + 2).start()

        @pl.when(z == 0)
        def _():
            @functools.partial(loop, 1, n_fsdp)
            def _(j):
                block = n_fsdp - j
                up_in[c, block] = own_part(c, block).astype(jnp.bfloat16)
                rise_copy(c, block).start()

        @pl.when(z == n_fsdp - 1)
        def _():
            @functools.partial(loop, 0, n_fsdp - 1)
            def _(block):
                down_in[c, block] = own_part(c, block).astype(jnp.bfloat16)
                fall_copy(c, block).start()

    def add_up(c):
        @pl.when((z > 0) & (z < n_fsdp - 1))
        def _():
            @functools.partial(loop, 1, n_fsdp)
            def _(j):
                block = n_fsdp - j

                @pl.when(block > z)
                def _():
                    copy = rise_copy(c, block)
                    copy.wait_recv()
                    summed = up_in[c, block].astype(jnp.float32) + own_part(c, block)
                    up_in[c, block] = summed.astype(jnp.bfloat16)
                    copy.start()

            @functools.partial(loop, 0, n_fsdp - 1)
            def _(block):
                @pl.when(block < z)
                def _():
                    copy = fall_copy(c, block)
                    copy.wait_recv()
                    summed = down_in[c, block].astype(jnp.float32) + own_part(c, block)
                    down_in[c, block] = summed.astype(jnp.bfloat16)
                    copy.start()

    def finish(c):
        def score(values):
            scored = values.astype(jnp.float32) * cot_t[c].astype(jnp.float32)
            for low in range(0, CHUNK, 128):
                total[...] += scored[:, low:low + 128]

        score(own_part(c, z))

        @pl.when(z > 0)
        def _():
            rise_copy(c, z).wait_recv()
            score(up_in[c, z])

        @pl.when(z < n_fsdp - 1)
        def _():
            fall_copy(c, z).wait_recv()
            score(down_in[c, z])

    total[...] = jnp.zeros_like(total)
    half = chunks // 2

    def computed(step):
        if step == chunks - 1:
            return chunks
        return max(0, min(step + 1, (step + 1 - half) * 5 // 2))

    for step in range(chunks):
        @functools.partial(loop, 1, n_fsdp)
        def _(k, step=step):
            pass_on(k, step)

        if step + AHEAD < chunks:
            start_own(step + AHEAD)
        if step == half - 1:
            c_pass(0)
        if step == half:
            c_pass(1)
            c_finish(0)
            turn()
            c_finish(1)
        done, before = computed(step - 1), computed(step - 2)
        loop(done, computed(step), compute)
        loop(before, done, add_up)
    last = computed(chunks - 2)
    loop(last, chunks, add_up)
    loop(0, chunks, finish)

    second[t] = jnp.sum(total[...].T.reshape(16, 8, depth_t), axis=0)

    def r2_copy(peer, owner, d):
        return remote(second.at[owner], second.at[owner], r2_send.at[d], r2_recv.at[owner],
                      {"tensor": peer})

    @functools.partial(loop, 1, n_tensor)
    def _(d):
        r2_copy(on_tensor(d), t, d).start()

    @functools.partial(loop, 1, n_tensor)
    def _(d):
        owner = on_tensor(d)
        r2_copy(owner, owner, d).wait_recv()

    out[...] = jnp.sum(jnp.sum(second[...], axis=0), axis=0, keepdims=True)

    @functools.partial(loop, 1, n_tensor)
    def _(d):
        peer = on_tensor(d)
        for copy in a_copies(peer, t, d) + (r2_copy(peer, t, d),):
            copy.wait_send()

    @functools.partial(loop, 1, n_fsdp)
    def _(d):
        peer = on_fsdp(d)
        for copy in b_copies(peer, z, d):
            copy.wait_send()

    for i in range(2):
        @functools.partial(loop, 1, pairs)
        def _(d, i=i):
            c_copy(i, same_core(d), t, c_send.at[i, d]).wait_send()

        @functools.partial(loop, 0, pairs)
        def _(d, i=i):
            owner = same_core(d)
            c_copy(i, twin, owner, twin_send.at[i, owner]).wait_send()

    @functools.partial(loop, 0, n_fsdp)
    def _(shard):
        @pl.when((shard <= z) & (z < n_fsdp - 1))
        def _():
            loop(0, chunks, lambda c: cot_copy(shard, c, up_send, above, False).wait_send())

        @pl.when((shard >= z) & (z > 0))
        def _():
            loop(0, chunks, lambda c: cot_copy(shard, c, down_send, below, False).wait_send())

        @pl.when(shard > z)
        def _():
            loop(0, chunks, lambda c: rise_copy(c, shard).wait_send())

        @pl.when(shard < z)
        def _():
            loop(0, chunks, lambda c: fall_copy(c, shard).wait_send())


def per_device(n_fsdp, n_tensor, val_x, val_cot, second_moment, train_x, train_cot):
    depth, depth_t = val_x.shape[0], train_x.shape[0]
    rows, hidden = second_moment.shape
    chunks = hidden // CHUNK
    width = val_x.shape[1] * n_tensor
    bf16, f32 = jnp.bfloat16, jnp.float32
    dma = pltpu.SemaphoreType.DMA
    scores = pl.pallas_call(
        functools.partial(kernel, n_fsdp, n_tensor),
        out_shape=jax.ShapeDtypeStruct((1, depth_t), f32),
        in_specs=[pl.BlockSpec(memory_space=pl.ANY)] * 5,
        out_specs=pl.BlockSpec(memory_space=pltpu.VMEM),
        scratch_shapes=[
            pltpu.VMEM((depth // n_tensor, width), bf16),
            pltpu.VMEM((depth_t // n_tensor, width), bf16),
            pltpu.VMEM((n_fsdp, depth, rows), bf16),
            pltpu.VMEM((n_fsdp, depth_t, rows), bf16),
            pltpu.VMEM((rows, n_fsdp * depth), bf16),
            pltpu.VMEM((chunks, n_fsdp * depth, CHUNK), bf16),
            pltpu.VMEM((chunks, depth_t, CHUNK), bf16),
            pltpu.VMEM((2, rows, CHUNK), f32),
            pltpu.VMEM((chunks, n_fsdp * depth_t, CHUNK), f32),
            pltpu.VMEM((depth_t, 128), f32),
            pltpu.VMEM((chunks, n_fsdp, depth_t, CHUNK), bf16),
            pltpu.VMEM((chunks, n_fsdp, depth_t, CHUNK), bf16),
            pltpu.VMEM((n_tensor, 8, depth_t), f32),
            dma((2, n_tensor)), dma((2, n_tensor)),
            dma((2, n_fsdp)), dma((2, n_fsdp)),
            dma((2, n_tensor)), dma((2, n_tensor)), dma((2, n_tensor)),
            dma((n_fsdp, chunks)), dma((n_fsdp, chunks)), dma((n_fsdp, chunks)),
            dma((chunks, n_fsdp)), dma((chunks, n_fsdp)),
            dma((chunks, n_fsdp)), dma((chunks, n_fsdp)),
            dma((2,)), dma((2, chunks)), dma((2,)),
            dma((n_tensor,)), dma((n_tensor,)),
        ],
        compiler_params=pltpu.CompilerParams(
            collective_id=0, has_side_effects=True, vmem_limit_bytes=60 * 1024 * 1024
        ),
        name="scores",
    )(val_x, val_cot, second_moment, train_x, train_cot)
    return scores.reshape(depth_t)


def solution(mesh):
    return jax.shard_map(
        functools.partial(per_device, mesh.shape["fsdp"], mesh.shape["tensor"]),
        mesh=mesh,
        in_specs=(P("fsdp", "tensor"),) * 5,
        out_specs=P("fsdp"),
        check_vma=False,
    )
```

```python
import functools

import jax
import jax.numpy as jnp
from jax import lax
from jax.experimental import pallas as pl
from jax.experimental.pallas import tpu as pltpu
from jax.sharding import PartitionSpec as P

EPSILON = 1e-08
CHUNK = 256
MESH = pl.DeviceIdType.MESH


def kernel(
    n_fsdp, n_tensor,
    val_x, val_cot, moment, train_x, train_cot, out,
    spread, spread_t, x_all, t_all, x_turned, cot, cot_t, moment_v, shifted, total,
    up_in, down_in, second,
    a_send, a_recv, b_send, b_recv, c_send, c_recv, twin_send, up_send, down_send, cot_recv,
    rise_send, rise_recv, fall_send, fall_recv,
    moment_sem, own_sem, local_sem, r2_send, r2_recv,
):
    z, t = lax.axis_index("fsdp"), lax.axis_index("tensor")
    chunks = cot.shape[0]
    depth, depth_t = val_cot.shape[0], train_cot.shape[0]
    rows, features = moment.shape[0], val_x.shape[1]
    share, share_t = spread.shape[0], spread_t.shape[0]

    def on_tensor(d):
        return lax.rem(t + d, n_tensor)

    def on_fsdp(d):
        return lax.rem(z + d, n_fsdp)

    def remote(src, dst, send, recv, device):
        return pltpu.make_async_remote_copy(
            src_ref=src, dst_ref=dst, send_sem=send, recv_sem=recv,
            device_id=device, device_id_type=MESH,
        )

    def loop(low, high, body):
        def step(i, carry):
            body(i)
            return carry
        lax.fori_loop(low, high, step, 0)

    barrier = pltpu.get_barrier_semaphore()

    @functools.partial(loop, 1, n_tensor)
    def _(d):
        pl.semaphore_signal(barrier, 1, device_id={"tensor": on_tensor(d)}, device_id_type=MESH)

    @functools.partial(loop, 1, n_fsdp)
    def _(d):
        pl.semaphore_signal(barrier, 1, device_id={"fsdp": on_fsdp(d)}, device_id_type=MESH)

    pl.semaphore_wait(barrier, n_tensor + n_fsdp - 2)

    def a_copies(peer, owner, d):
        columns = pl.ds(pl.multiple_of(owner * features, features), features)
        return (
            remote(val_x.at[pl.ds(pl.multiple_of(peer * share, share), share)],
                   spread.at[:, columns], a_send.at[0, d], a_recv.at[0, owner], {"tensor": peer}),
            remote(train_x.at[pl.ds(pl.multiple_of(peer * share_t, share_t), share_t)],
                   spread_t.at[:, columns], a_send.at[1, d], a_recv.at[1, owner], {"tensor": peer}),
        )

    def a_own():
        columns = pl.ds(pl.multiple_of(t * features, features), features)
        return (
            pltpu.make_async_copy(val_x.at[pl.ds(pl.multiple_of(t * share, share), share)],
                                  spread.at[:, columns], local_sem.at[0]),
            pltpu.make_async_copy(train_x.at[pl.ds(pl.multiple_of(t * share_t, share_t), share_t)],
                                  spread_t.at[:, columns], local_sem.at[1]),
        )

    def b_copies(peer, owner, d):
        columns = pl.ds(pl.multiple_of(peer * rows, rows), rows)
        return (
            remote(spread.at[:, columns],
                   x_all.at[owner, pl.ds(pl.multiple_of(t * share, share), share)],
                   b_send.at[0, d], b_recv.at[0, owner], {"fsdp": peer}),
            remote(spread_t.at[:, columns],
                   t_all.at[owner, pl.ds(pl.multiple_of(t * share_t, share_t), share_t)],
                   b_send.at[1, d], b_recv.at[1, owner], {"fsdp": peer}),
        )

    def b_own():
        columns = pl.ds(pl.multiple_of(z * rows, rows), rows)
        return (
            pltpu.make_async_copy(
                spread.at[:, columns],
                x_all.at[z, pl.ds(pl.multiple_of(t * share, share), share)], local_sem.at[0]),
            pltpu.make_async_copy(
                spread_t.at[:, columns],
                t_all.at[z, pl.ds(pl.multiple_of(t * share_t, share_t), share_t)],
                local_sem.at[1]),
        )

    core = lax.rem(t, 2)
    twin = t + 1 - 2 * core
    pairs = n_tensor // 2

    def same_core(d):
        return 2 * lax.rem(t // 2 + d, pairs) + core

    def c_copy(i, peer, owner, sem):
        held, size = ((x_all, share), (t_all, share_t))[i]
        piece = pl.ds(pl.multiple_of(owner * size, size), size)
        return remote(held.at[:, piece], held.at[:, piece], sem, c_recv.at[i, owner],
                      {"tensor": peer})

    def c_start(i):
        @functools.partial(loop, 1, pairs)
        def _(d):
            c_copy(i, same_core(d), t, c_send.at[i, d]).start()

        c_copy(i, twin, t, twin_send.at[i, t]).start()

    def c_pass(i):
        @functools.partial(loop, 1, pairs)
        def _(d):
            owner = same_core(d)
            c_copy(i, owner, owner, c_send.at[i, d]).wait_recv()
            c_copy(i, twin, owner, twin_send.at[i, owner]).start()

    def c_finish(i):
        @functools.partial(loop, 0, pairs)
        def _(d):
            owner = same_core(d) + 1 - 2 * core
            c_copy(i, twin, owner, twin_send.at[i, owner]).wait_recv()

    def cot_copy(shard, c, sems, peer, own):
        place = cot.at[c, pl.ds(pl.multiple_of(shard * depth, depth), depth)]
        columns = pl.ds(pl.multiple_of(c * CHUNK, CHUNK), CHUNK)
        return remote(val_cot.at[:, columns] if own else place, place,
                      sems.at[shard, c], cot_recv.at[shard, c], {"fsdp": peer})

    below, above = lax.max(z - 1, 0), lax.min(z + 1, n_fsdp - 1)

    def start_own(c):
        @pl.when(z < n_fsdp - 1)
        def _():
            cot_copy(z, c, up_send, above, True).start()

        @pl.when(z > 0)
        def _():
            cot_copy(z, c, down_send, below, True).start()

    def cot_own(c):
        columns = pl.ds(pl.multiple_of(c * CHUNK, CHUNK), CHUNK)
        place = cot.at[c, pl.ds(pl.multiple_of(z * depth, depth), depth)]
        return (
            pltpu.make_async_copy(val_cot.at[:, columns], place, own_sem.at[0, c]),
            pltpu.make_async_copy(train_cot.at[:, columns], cot_t.at[c], own_sem.at[1, c]),
        )

    def moment_copy(c):
        columns = pl.ds(pl.multiple_of(c * CHUNK, CHUNK), CHUNK)
        return pltpu.make_async_copy(moment.at[:, columns], moment_v.at[lax.rem(c, 2)],
                                     moment_sem.at[lax.rem(c, 2)])

    @functools.partial(loop, 1, n_tensor)
    def _(d):
        for copy in a_copies(on_tensor(d), t, d):
            copy.start()

    for copy in a_own():
        copy.start()
    start_own(0)

    @functools.partial(loop, 1, n_tensor)
    def _(d):
        owner = on_tensor(d)
        for copy in a_copies(owner, owner, d):
            copy.wait_recv()

    for copy in a_own():
        copy.wait()

    @functools.partial(loop, 1, n_fsdp)
    def _(d):
        for copy in b_copies(on_fsdp(d), z, d):
            copy.start()

    for copy in b_own():
        copy.start()
    loop(1, chunks, start_own)

    @functools.partial(loop, 0, chunks)
    def _(c):
        for copy in cot_own(c):
            copy.start()

    for c in range(2):
        moment_copy(c).start()

    @functools.partial(loop, 1, n_fsdp)
    def _(d):
        owner = on_fsdp(d)
        for copy in b_copies(owner, owner, d):
            copy.wait_recv()

    for copy in b_own():
        copy.wait()

    c_start(0)
    c_start(1)

    def pass_on(k, c):
        lower, upper = z - k, z + k

        @pl.when(lower >= 0)
        def _():
            copy = cot_copy(lower, c, up_send, above, False)
            copy.wait_recv()

            @pl.when(z < n_fsdp - 1)
            def _():
                copy.start()

        @pl.when(upper < n_fsdp)
        def _():
            copy = cot_copy(upper, c, down_send, below, False)
            copy.wait_recv()

            @pl.when(z > 0)
            def _():
                copy.start()

    tile = min(512, rows)

    def turn():
        @functools.partial(loop, 0, rows // tile)
        def _(i):
            columns = pl.ds(pl.multiple_of(i * tile, tile), tile)
            for group in range(n_fsdp):
                x_turned[columns, group * depth:(group + 1) * depth] = x_all[group, :, columns].T

    def rise_copy(c, block):
        return remote(up_in.at[c, block], up_in.at[c, block],
                      rise_send.at[c, block], rise_recv.at[c, block], {"fsdp": above})

    def fall_copy(c, block):
        return remote(down_in.at[c, block], down_in.at[c, block],
                      fall_send.at[c, block], fall_recv.at[c, block], {"fsdp": below})

    def own_part(c, block):
        return shifted[c, pl.ds(pl.multiple_of(block * depth_t, depth_t), depth_t), :]

    def compute(c):
        for copy in cot_own(c):
            copy.wait()
        moment_copy(c).wait()
        shifted[c] = jnp.zeros(shifted.shape[1:], jnp.float32)

        @functools.partial(loop, 0, rows // tile)
        def _(i):
            block = pl.ds(pl.multiple_of(i * tile, tile), tile)
            grad = jnp.dot(x_turned[block, :], cot[c], preferred_element_type=jnp.float32)
            root = jnp.sqrt(moment_v[lax.rem(c, 2), block, :]) + EPSILON
            delta = (grad / root).astype(jnp.bfloat16)
            lhs = t_all[:, :, block].reshape(n_fsdp * depth_t, tile)
            shifted[c] += jnp.dot(lhs, delta, preferred_element_type=jnp.float32)

        @pl.when(c + 2 < chunks)
        def _():
            moment_copy(c + 2).start()

        @pl.when(z == 0)
        def _():
            @functools.partial(loop, 1, n_fsdp)
            def _(j):
                block = n_fsdp - j
                up_in[c, block] = own_part(c, block).astype(jnp.bfloat16)
                rise_copy(c, block).start()

        @pl.when(z == n_fsdp - 1)
        def _():
            @functools.partial(loop, 0, n_fsdp - 1)
            def _(block):
                down_in[c, block] = own_part(c, block).astype(jnp.bfloat16)
                fall_copy(c, block).start()

    def add_up(c):
        @pl.when((z > 0) & (z < n_fsdp - 1))
        def _():
            @functools.partial(loop, 1, n_fsdp)
            def _(j):
                block = n_fsdp - j

                @pl.when(block > z)
                def _():
                    copy = rise_copy(c, block)
                    copy.wait_recv()
                    summed = up_in[c, block].astype(jnp.float32) + own_part(c, block)
                    up_in[c, block] = summed.astype(jnp.bfloat16)
                    copy.start()

            @functools.partial(loop, 0, n_fsdp - 1)
            def _(block):
                @pl.when(block < z)
                def _():
                    copy = fall_copy(c, block)
                    copy.wait_recv()
                    summed = down_in[c, block].astype(jnp.float32) + own_part(c, block)
                    down_in[c, block] = summed.astype(jnp.bfloat16)
                    copy.start()

    def finish(c):
        def score(values):
            scored = values.astype(jnp.float32) * cot_t[c].astype(jnp.float32)
            for low in range(0, CHUNK, 128):
                total[...] += scored[:, low:low + 128]

        score(own_part(c, z))

        @pl.when(z > 0)
        def _():
            rise_copy(c, z).wait_recv()
            score(up_in[c, z])

        @pl.when(z < n_fsdp - 1)
        def _():
            fall_copy(c, z).wait_recv()
            score(down_in[c, z])

    total[...] = jnp.zeros_like(total)

    loop(0, chunks, lambda c: pass_on(1, c))
    c_pass(0)
    c_pass(1)

    @functools.partial(loop, 2, n_fsdp - 1)
    def _(k):
        loop(0, chunks, lambda c: pass_on(k, c))

    c_finish(0)
    c_finish(1)
    turn()

    @functools.partial(loop, 0, chunks)
    def _(c):
        pass_on(n_fsdp - 1, c)
        compute(c)

        @pl.when(c > 0)
        def _():
            add_up(c - 1)

    add_up(chunks - 1)
    loop(0, chunks, finish)

    second[t] = jnp.sum(total[...].T.reshape(16, 8, depth_t), axis=0)

    def r2_copy(peer, owner, d):
        return remote(second.at[owner], second.at[owner], r2_send.at[d], r2_recv.at[owner],
                      {"tensor": peer})

    @functools.partial(loop, 1, n_tensor)
    def _(d):
        r2_copy(on_tensor(d), t, d).start()

    @functools.partial(loop, 1, n_tensor)
    def _(d):
        owner = on_tensor(d)
        r2_copy(owner, owner, d).wait_recv()

    out[...] = jnp.sum(jnp.sum(second[...], axis=0), axis=0, keepdims=True)

    @functools.partial(loop, 1, n_tensor)
    def _(d):
        peer = on_tensor(d)
        for copy in a_copies(peer, t, d) + (r2_copy(peer, t, d),):
            copy.wait_send()

    @functools.partial(loop, 1, n_fsdp)
    def _(d):
        peer = on_fsdp(d)
        for copy in b_copies(peer, z, d):
            copy.wait_send()

    for i in range(2):
        @functools.partial(loop, 1, pairs)
        def _(d, i=i):
            c_copy(i, same_core(d), t, c_send.at[i, d]).wait_send()

        @functools.partial(loop, 0, pairs)
        def _(d, i=i):
            owner = same_core(d)
            c_copy(i, twin, owner, twin_send.at[i, owner]).wait_send()

    @functools.partial(loop, 0, n_fsdp)
    def _(shard):
        @pl.when((shard <= z) & (z < n_fsdp - 1))
        def _():
            loop(0, chunks, lambda c: cot_copy(shard, c, up_send, above, False).wait_send())

        @pl.when((shard >= z) & (z > 0))
        def _():
            loop(0, chunks, lambda c: cot_copy(shard, c, down_send, below, False).wait_send())

        @pl.when(shard > z)
        def _():
            loop(0, chunks, lambda c: rise_copy(c, shard).wait_send())

        @pl.when(shard < z)
        def _():
            loop(0, chunks, lambda c: fall_copy(c, shard).wait_send())


def per_device(n_fsdp, n_tensor, val_x, val_cot, second_moment, train_x, train_cot):
    depth, depth_t = val_x.shape[0], train_x.shape[0]
    rows, hidden = second_moment.shape
    chunks = hidden // CHUNK
    width = val_x.shape[1] * n_tensor
    bf16, f32 = jnp.bfloat16, jnp.float32
    dma = pltpu.SemaphoreType.DMA
    scores = pl.pallas_call(
        functools.partial(kernel, n_fsdp, n_tensor),
        out_shape=jax.ShapeDtypeStruct((1, depth_t), f32),
        in_specs=[pl.BlockSpec(memory_space=pl.ANY)] * 5,
        out_specs=pl.BlockSpec(memory_space=pltpu.VMEM),
        scratch_shapes=[
            pltpu.VMEM((depth // n_tensor, width), bf16),
            pltpu.VMEM((depth_t // n_tensor, width), bf16),
            pltpu.VMEM((n_fsdp, depth, rows), bf16),
            pltpu.VMEM((n_fsdp, depth_t, rows), bf16),
            pltpu.VMEM((rows, n_fsdp * depth), bf16),
            pltpu.VMEM((chunks, n_fsdp * depth, CHUNK), bf16),
            pltpu.VMEM((chunks, depth_t, CHUNK), bf16),
            pltpu.VMEM((2, rows, CHUNK), f32),
            pltpu.VMEM((chunks, n_fsdp * depth_t, CHUNK), f32),
            pltpu.VMEM((depth_t, 128), f32),
            pltpu.VMEM((chunks, n_fsdp, depth_t, CHUNK), bf16),
            pltpu.VMEM((chunks, n_fsdp, depth_t, CHUNK), bf16),
            pltpu.VMEM((n_tensor, 8, depth_t), f32),
            dma((2, n_tensor)), dma((2, n_tensor)),
            dma((2, n_fsdp)), dma((2, n_fsdp)),
            dma((2, n_tensor)), dma((2, n_tensor)), dma((2, n_tensor)),
            dma((n_fsdp, chunks)), dma((n_fsdp, chunks)), dma((n_fsdp, chunks)),
            dma((chunks, n_fsdp)), dma((chunks, n_fsdp)),
            dma((chunks, n_fsdp)), dma((chunks, n_fsdp)),
            dma((2,)), dma((2, chunks)), dma((2,)),
            dma((n_tensor,)), dma((n_tensor,)),
        ],
        compiler_params=pltpu.CompilerParams(
            collective_id=0, has_side_effects=True, vmem_limit_bytes=60 * 1024 * 1024
        ),
        name="scores",
    )(val_x, val_cot, second_moment, train_x, train_cot)
    return scores.reshape(depth_t)


def solution(mesh):
    return jax.shard_map(
        functools.partial(per_device, mesh.shape["fsdp"], mesh.shape["tensor"]),
        mesh=mesh,
        in_specs=(P("fsdp", "tensor"),) * 5,
        out_specs=P("fsdp"),
        check_vma=False,
    )
```
